256 devices in a mesh: gx: 16 (over z, core), gy: 16 (over y, x).
Axes of the slice: x: 4, y: 4, z: 8, core: 2. Of those that a mesh axis runs over, the one named last changes fastest.
Arguments:
- tokens: bfloat16 [128, 8192], P(None, 'gx'), may hold values from -150 to 150
- norm_gain: float32 [8192], P('gx'), may hold values from 0.25 to 1.75
- w_project: bfloat16 [8192, 4, 8192], P('gx', None, 'gy'), may hold values from -0.0625 to 0.0625
- w_output: bfloat16 [8192, 8192], P('gy', 'gx'), may hold values from -0.0625 to 0.0625
- decay: float32 [32], P('gy'), may hold values from 0.5 to 0.99
- state: float32 [128, 32, 256, 256], P('gx', 'gy'), may hold values from -3 to 3
Outputs:
- mixed: bfloat16 [128, 8192], P(None, 'gx')
- new_state: float32 [128, 32, 256, 256], P('gx', 'gy')
The draws below stay inside these ranges and needn't reach their ends.
All inputs are finite; a program needn't handle non-finite values.
Results may differ from the reference program's by a relative error of at most 0.009.
Values may be sent and summed in bfloat16 or wider, within the bound.
No kernel may reach another device: no remote copies, remote signals or barrier semaphores. Data moves between devices by JAX's collectives and lax.ppermute only.
A program may use at most 64 MiB of HBM per device.

```python
import jax
import jax.numpy as jnp
from jax import lax

H = 32
HS = 256
D = 8192
SEQ = 128


def draw_tokens(key, part):
    key = jax.random.fold_in(key, 11)
    key_noise, key_rows, key_cols = jax.random.split(key, 3)
    noise = jax.random.normal(key_noise, (SEQ, D), jnp.float32)
    row_scale = jnp.power(10.0, jax.random.uniform(key_rows, (SEQ, 1), jnp.float32))
    col_scale = jnp.power(10.0, jax.random.uniform(key_cols, (1, D), jnp.float32))
    where = jnp.arange(D, dtype=jnp.float32)[None, :] / D
    ramp = jnp.power(3.0, 0.5 * where)
    noise = jnp.clip(noise, -4.0, 4.0)
    return (noise * row_scale * col_scale * ramp / 8.0).astype(jnp.bfloat16)


def block_levels(rng, shape, cuts, least, largest):
    gain, own = 1.0, jax.random.fold_in(rng, 6)
    for dim, blocks in cuts:
        heights = jnp.exp(jax.random.uniform(jax.random.fold_in(own, dim), (blocks,), jnp.float32, least / len(cuts), largest / len(cuts)))
        gain = gain * jnp.repeat(heights, shape[dim] // blocks).reshape([-1 if axis == dim else 1 for axis in range(len(shape))])
    return gain


def normal_values(stream_key, extent, scale, reach, cuts=(), kind=jnp.bfloat16):
    drawn = scale * jax.random.normal(stream_key, extent, jnp.float32)
    if cuts:
        drawn = drawn * block_levels(stream_key, extent, cuts, -0.22, 0.18)
    return jnp.clip(drawn, -reach, reach).astype(kind)


def setup_inputs(seed: int = 0) -> dict:
    keys = jax.random.split(jax.random.key(seed), 7)
    tokens = draw_tokens(jax.random.fold_in(keys[6], 71), 0)
    norm_gain = jnp.clip(1.0 + 0.15 * jax.random.normal(keys[1], (D,), jnp.float32), 0.25, 1.75)
    w_project = normal_values(keys[2], (D, 4, D), D ** -0.5, 0.0625, ((0, 16), (2, 16)))
    w_output = normal_values(keys[3], (D, D), D ** -0.5, 0.0625, ((0, 16), (1, 16)))
    decay = jnp.clip(0.5 + 0.49 * jax.random.uniform(keys[4], (H,), jnp.float32) ** block_levels(keys[4], (H,), ((0, 16),), -0.2, 0.2), 0.5, 0.99)
    state = normal_values(keys[5], (SEQ, H, HS, HS), 0.5, 3.0, ((0, 16), (1, 16)), jnp.float32)
    return {"tokens": tokens, "norm_gain": norm_gain, "w_project": w_project, "w_output": w_output, "decay": decay, "state": state}


def reference(tokens, norm_gain, w_project, w_output, decay, state):
    tokens_f = tokens.astype(jnp.float32)
    inverse_rms = lax.rsqrt(lax.optimization_barrier(jnp.mean(tokens_f * tokens_f, axis=1)) + 1e-06)
    scaled_in = (tokens_f * norm_gain.astype(jnp.float32)).astype(jnp.bfloat16)
    summed = jnp.dot(scaled_in, w_project.reshape(D, 4 * D), preferred_element_type=jnp.float32)
    projected = (summed * inverse_rms[:, None]).reshape(SEQ, 4, H, HS)
    query = projected[:, 0]
    keys_scaled = projected[:, 1] * HS ** (-0.5)
    values = projected[:, 2]
    gates = projected[:, 3].reshape(SEQ, D)
    new_state = decay.astype(jnp.float32)[None, :, None, None] * state + keys_scaled[:, :, :, None] * values[:, :, None, :]
    readout = jnp.einsum('shk,shkv->shv', query, new_state, precision=lax.Precision.HIGHEST)
    centre = lax.optimization_barrier(jnp.mean(readout, axis=2, keepdims=True))
    spread = lax.optimization_barrier(jnp.mean((readout - centre) ** 2, axis=2, keepdims=True))
    normed = (readout - centre) * lax.rsqrt(spread + 1e-05)
    gated = (jax.nn.silu(gates) * normed.reshape(SEQ, D)).astype(jnp.bfloat16)
    mixed = (tokens_f + jnp.dot(gated, w_output, preferred_element_type=jnp.float32)).astype(jnp.bfloat16)
    return (mixed, new_state)
```

```python
import jax
import jax.numpy as jnp
from jax import lax
from jax.experimental import pallas as pl
from jax.experimental.pallas import tpu as pltpu
from jax.sharding import PartitionSpec as P

HS = 256
D = 8192
LANES = 128


def state_kernel(decay_ref, parts_ref, state_ref, new_ref, gated_ref, cols_ref):
    pieces, rows, _ = parts_ref.shape
    heads = state_ref.shape[1]
    width = heads * HS
    summed = parts_ref[0].astype(jnp.float32)
    for z in range(1, pieces):
        summed += parts_ref[z].astype(jnp.float32)
    squares = summed[:, 4 * width : 4 * width + 1] + summed[:, 4 * width + 1 : 4 * width + 2]
    scale = lax.rsqrt(squares / D + 1e-06)
    projected = summed[:, : 4 * width] * scale
    queries = projected[:, :width]
    keys = projected[:, width : 2 * width] * HS ** (-0.5)
    values = projected[:, 2 * width : 3 * width]
    gates = projected[:, 3 * width : 4 * width]
    cols_ref[0] = queries.T
    cols_ref[1] = keys.T
    readouts = []
    for h in range(heads):
        decay = decay_ref[h]
        per_head = []
        for s in range(rows):
            key_col = cols_ref[1, h * HS : (h + 1) * HS, s : s + 1]
            query_col = cols_ref[0, h * HS : (h + 1) * HS, s : s + 1]
            value_row = values[s : s + 1, h * HS : (h + 1) * HS]
            updated = decay * state_ref[s, h] + key_col * value_row
            new_ref[s, h] = updated
            per_head.append(jnp.sum(query_col * updated, axis=0, keepdims=True))
        readout = jnp.concatenate(per_head, axis=0)
        centre = jnp.mean(readout, axis=1, keepdims=True)
        spread = jnp.mean((readout - centre) ** 2, axis=1, keepdims=True)
        readouts.append((readout - centre) * lax.rsqrt(spread + 1e-05))
    normed = jnp.concatenate(readouts, axis=1)
    gated = gates / (1.0 + jnp.exp(-gates)) * normed
    gated_ref[...] = gated.astype(jnp.bfloat16)


def local(tokens, norm_gain, w_project, w_output, decay, state):
    all_rows, features = tokens.shape
    size_x, size_y = lax.axis_size("gx"), lax.axis_size("gy")
    chips = size_x // 2
    own_rows = all_rows // size_x
    out_rows = all_rows // size_y
    core = lax.axis_index("gx") % 2
    tokens_f = tokens.astype(jnp.float32)
    scaled_in = (tokens_f * norm_gain).astype(jnp.bfloat16)
    squares = jnp.sum(tokens_f * tokens_f, axis=1, keepdims=True)
    flat_weights = w_project.reshape(features, -1)
    x_split = scaled_in.reshape(chips, 2, own_rows, features)
    s_split = squares.reshape(chips, 2, own_rows, 1)

    def project(which):
        x = lax.dynamic_index_in_dim(x_split, which, 1, False).reshape(-1, features)
        s = lax.dynamic_index_in_dim(s_split, which, 1, False).reshape(-1, 1)
        return jnp.dot(x, flat_weights, preferred_element_type=jnp.float32), s

    def pack(sums, squares):
        high = squares.astype(jnp.bfloat16)
        low = (squares - high.astype(jnp.float32)).astype(jnp.bfloat16)
        tail = jnp.concatenate([high, low], axis=1)
        tail = jnp.pad(tail, ((0, 0), (0, LANES - 2)))
        return jnp.concatenate([sums.astype(jnp.bfloat16), tail], axis=1)

    away = pack(*project(1 - core))
    arrived = lax.ppermute(away, "gx", [(i, i ^ 1) for i in range(size_x)]).astype(jnp.float32)
    sums, own_squares = project(core)
    width = sums.shape[1]
    pair = pack(
        sums + arrived[:, :width],
        own_squares + arrived[:, width : width + 1] + arrived[:, width + 1 : width + 2],
    )
    groups = [[2 * z + c for z in range(chips)] for c in range(2)]
    parts = lax.all_to_all(
        pair.reshape(chips, own_rows, -1), "gx", 0, 0, axis_index_groups=groups
    )
    new_state, gated = pl.pallas_call(
        state_kernel,
        out_shape=(
            jax.ShapeDtypeStruct(state.shape, jnp.float32),
            jax.ShapeDtypeStruct((own_rows, state.shape[1] * HS), jnp.bfloat16),
        ),
        in_specs=[
            pl.BlockSpec(memory_space=pltpu.SMEM),
            pl.BlockSpec(memory_space=pltpu.VMEM),
            pl.BlockSpec(memory_space=pltpu.VMEM),
        ],
        out_specs=(
            pl.BlockSpec(memory_space=pltpu.VMEM),
            pl.BlockSpec(memory_space=pltpu.VMEM),
        ),
        scratch_shapes=[pltpu.VMEM((2, state.shape[1] * HS, own_rows), jnp.float32)],
        compiler_params=pltpu.CompilerParams(vmem_limit_bytes=24 * 2**20),
        name="retention",
    )(decay, parts, state)
    copies = jnp.broadcast_to(gated[None], (size_x,) + gated.shape)
    all_gated = lax.all_to_all(copies, "gx", 0, 0).reshape(all_rows, -1)
    head_terms = jnp.dot(all_gated, w_output, preferred_element_type=jnp.float32)
    terms = lax.all_to_all(
        head_terms.astype(jnp.bfloat16).reshape(size_y, out_rows, -1), "gy", 0, 0
    )
    own_tokens = lax.dynamic_slice_in_dim(tokens_f, lax.axis_index("gy") * out_rows, out_rows, 0)
    own_mixed = (own_tokens + jnp.sum(terms.astype(jnp.float32), axis=0)).astype(jnp.bfloat16)
    copies = jnp.broadcast_to(own_mixed[None], (size_y,) + own_mixed.shape)
    mixed = lax.all_to_all(copies, "gy", 0, 0).reshape(all_rows, -1)
    return (mixed, new_state)


def solution(mesh):
    placed = (
        P(None, "gx"),
        P("gx"),
        P("gx", None, "gy"),
        P("gy", "gx"),
        P("gy"),
        P("gx", "gy", None, None),
    )
    return jax.shard_map(
        local,
        mesh=mesh,
        in_specs=placed,
        out_specs=(P(None, "gx"), P("gx", "gy", None, None)),
        check_vma=False,
    )
```

```python
import jax
import jax.numpy as jnp
from jax import lax
from jax.experimental import pallas as pl
from jax.experimental.pallas import tpu as pltpu
from jax.sharding import PartitionSpec as P

HS = 256
D = 8192
LANES = 128


def split_squares(squares):
    high = squares.astype(jnp.bfloat16).astype(jnp.float32)
    low = squares - high
    lane = lax.broadcasted_iota(jnp.int32, (squares.shape[0], LANES), 1)
    return jnp.where(lane == 0, high, jnp.where(lane == 1, low, 0.0))


def project_kernel(
    tokens_ref, gain_ref, weights_ref, away_ref, own_ref, kept_ref, scaled_ref, squares_ref
):
    chips, _, rows, features = scaled_ref.shape
    core = lax.rem(lax.axis_index("gx"), 2)
    tokens = tokens_ref[...].astype(jnp.float32)
    squares = jnp.sum(tokens * tokens, axis=1, keepdims=True)
    scaled_ref[...] = (tokens * gain_ref[...]).reshape(scaled_ref.shape)
    squares_ref[...] = jnp.broadcast_to(squares, (tokens.shape[0], LANES)).reshape(squares_ref.shape)
    block = lax.axis_index("gy")
    kept = jnp.zeros(kept_ref.shape, jnp.float32)
    for y in range(tokens.shape[0] // kept.shape[0]):
        kept = jnp.where(block == y, tokens[y * kept.shape[0] : (y + 1) * kept.shape[0]], kept)
    kept_ref[...] = kept
    width = weights_ref.shape[1]
    half = chips * rows
    x = jnp.concatenate(
        [scaled_ref[:, which].reshape(half, features) for which in (1 - core, core)], axis=0
    ).astype(jnp.bfloat16)
    sums = jnp.dot(x, weights_ref[...], preferred_element_type=jnp.float32)
    for n, (which, out_ref) in enumerate(((1 - core, away_ref), (core, own_ref))):
        out_ref[:, :width] = sums[n * half : (n + 1) * half].astype(out_ref.dtype)
        total = squares_ref[:, which].reshape(half, LANES)[:, :1]
        out_ref[:, width:] = split_squares(total).astype(out_ref.dtype)


def pair_kernel(own_ref, arrived_ref, state_ref, pair_ref):
    del state_ref
    width = own_ref.shape[1] - LANES
    pair_ref[:, :width] = (
        own_ref[:, :width] + arrived_ref[:, :width].astype(jnp.float32)
    ).astype(jnp.bfloat16)
    tail = own_ref[:, width:] + arrived_ref[:, width:].astype(jnp.float32)
    total = tail[:, 0:1] + tail[:, 1:2]
    pair_ref[:, width:] = split_squares(total).astype(jnp.bfloat16)


def readout_kernel(
    decay_ref, parts_ref, state_ref, copies_ref, key_cols_ref, values_ref, query_cols_ref
):
    pieces, rows, _ = parts_ref.shape
    heads = state_ref.shape[1]
    width = heads * HS
    summed = parts_ref[0].astype(jnp.float32)
    for z in range(1, pieces):
        summed += parts_ref[z].astype(jnp.float32)
    squares = summed[:, 4 * width : 4 * width + 1] + summed[:, 4 * width + 1 : 4 * width + 2]
    scale = lax.rsqrt(squares / D + 1e-06)
    projected = summed[:, : 4 * width] * scale
    queries = projected[:, :width]
    keys = projected[:, width : 2 * width] * HS ** (-0.5)
    values = projected[:, 2 * width : 3 * width]
    gates = projected[:, 3 * width : 4 * width]
    query_cols_ref[...] = queries.T
    key_cols_ref[...] = keys.T
    values_ref[...] = values
    from_state = [[] for _ in range(heads)]
    for s in range(rows):
        for h in range(heads):
            query_col = query_cols_ref[h * HS : (h + 1) * HS, s : s + 1]
            from_state[h].append(jnp.sum(query_col * state_ref[s, h], axis=0, keepdims=True))
    normed = []
    for h in range(heads):
        here = slice(h * HS, (h + 1) * HS)
        overlap = jnp.sum(queries[:, here] * keys[:, here], axis=1, keepdims=True)
        readout = (
            decay_ref[h] * jnp.concatenate(from_state[h], axis=0) + overlap * values[:, here]
        )
        centre = jnp.mean(readout, axis=1, keepdims=True)
        spread = jnp.mean((readout - centre) ** 2, axis=1, keepdims=True)
        normed.append((readout - centre) * lax.rsqrt(spread + 1e-05))
    gated = gates / (1.0 + jnp.exp(-gates)) * jnp.concatenate(normed, axis=1)
    copies_ref[...] = jnp.broadcast_to(gated.astype(jnp.bfloat16)[None], copies_ref.shape)


def update_kernel(
    decay_ref, key_cols_ref, values_ref, state_ref, new_ref, held_ref, fresh_ref, in_sems, out_sems
):
    rows, heads = state_ref.shape[:2]
    loads = [
        pltpu.make_async_copy(state_ref.at[s], held_ref.at[s], in_sems.at[s]) for s in range(rows)
    ]
    stores = [
        pltpu.make_async_copy(fresh_ref.at[s], new_ref.at[s], out_sems.at[s]) for s in range(rows)
    ]
    for load in loads:
        load.start()
    for s in range(rows):
        loads[s].wait()
        for h in range(heads):
            key_col = key_cols_ref[h * HS : (h + 1) * HS, s : s + 1]
            value_row = values_ref[s : s + 1, h * HS : (h + 1) * HS]
            fresh_ref[s, h] = decay_ref[h] * held_ref[s, h] + key_col * value_row
        stores[s].start()
    for store in stores:
        store.wait()


def finish_kernel(kept_ref, terms_ref, copies_ref):
    total = terms_ref[0].astype(jnp.float32)
    for y in range(1, terms_ref.shape[0]):
        total += terms_ref[y].astype(jnp.float32)
    mixed = (kept_ref[...] + total).astype(jnp.bfloat16)
    copies_ref[...] = jnp.broadcast_to(mixed[None], copies_ref.shape)


def local(tokens, norm_gain, w_project, w_output, decay, state):
    all_rows, features = tokens.shape
    size_x, size_y = lax.axis_size("gx"), lax.axis_size("gy")
    chips = size_x // 2
    own_rows = all_rows // size_x
    out_rows = all_rows // size_y
    heads = state.shape[1]
    flat_weights = w_project.reshape(features, -1)
    padded = flat_weights.shape[1] + LANES
    half = all_rows // 2
    vmem = pl.BlockSpec(memory_space=pltpu.VMEM)
    smem = pl.BlockSpec(memory_space=pltpu.SMEM)
    hbm = pl.BlockSpec(memory_space=pltpu.HBM)
    away, own, kept = pl.pallas_call(
        project_kernel,
        out_shape=(
            jax.ShapeDtypeStruct((half, padded), jnp.bfloat16),
            jax.ShapeDtypeStruct((half, padded), jnp.float32),
            pltpu.VMEM((out_rows, features), jnp.float32),
        ),
        in_specs=[vmem, vmem, vmem],
        out_specs=(vmem, vmem, vmem),
        scratch_shapes=[
            pltpu.VMEM((chips, 2, own_rows, features), jnp.float32),
            pltpu.VMEM((chips, 2, own_rows, LANES), jnp.float32),
        ],
        compiler_params=pltpu.CompilerParams(vmem_limit_bytes=16 * 2**20),
        name="project",
    )(tokens, norm_gain.reshape(1, -1), flat_weights)
    state_hbm = pltpu.with_memory_space_constraint(state, pltpu.HBM)
    arrived = lax.ppermute(away, "gx", [(i, i ^ 1) for i in range(size_x)])
    pair = pl.pallas_call(
        pair_kernel,
        out_shape=jax.ShapeDtypeStruct((half, padded), jnp.bfloat16),
        in_specs=[vmem, vmem, pl.BlockSpec(memory_space=pl.ANY)],
        out_specs=vmem,
        compiler_params=pltpu.CompilerParams(vmem_limit_bytes=16 * 2**20),
        name="pair",
    )(own, arrived, state)
    groups = [[2 * z + c for z in range(chips)] for c in range(2)]
    parts = lax.all_to_all(
        pair.reshape(chips, own_rows, -1), "gx", 0, 0, axis_index_groups=groups
    )
    copies, key_cols, values = pl.pallas_call(
        readout_kernel,
        out_shape=(
            jax.ShapeDtypeStruct((size_x, own_rows, heads * HS), jnp.bfloat16),
            jax.ShapeDtypeStruct((heads * HS, own_rows), jnp.float32),
            jax.ShapeDtypeStruct((own_rows, heads * HS), jnp.float32),
        ),
        in_specs=[smem, vmem, vmem],
        out_specs=(vmem, vmem, vmem),
        scratch_shapes=[pltpu.VMEM((heads * HS, own_rows), jnp.float32)],
        compiler_params=pltpu.CompilerParams(vmem_limit_bytes=24 * 2**20),
        name="readout",
    )(decay, parts, state)
    new_state = pl.pallas_call(
        update_kernel,
        out_shape=jax.ShapeDtypeStruct(state.shape, jnp.float32),
        in_specs=[smem, vmem, vmem, hbm],
        out_specs=hbm,
        scratch_shapes=[
            pltpu.VMEM(state.shape, jnp.float32),
            pltpu.VMEM(state.shape, jnp.float32),
            pltpu.SemaphoreType.DMA((own_rows,)),
            pltpu.SemaphoreType.DMA((own_rows,)),
        ],
        compiler_params=pltpu.CompilerParams(vmem_limit_bytes=24 * 2**20),
        cost_estimate=pl.CostEstimate(flops=2**22, bytes_accessed=2**23, transcendentals=0),
        name="update",
    )(decay, key_cols, values, state_hbm)
    all_gated = lax.all_to_all(copies, "gx", 0, 0).reshape(all_rows, -1)
    head_terms = jnp.dot(all_gated, w_output, preferred_element_type=jnp.float32)
    terms = lax.all_to_all(
        head_terms.astype(jnp.bfloat16).reshape(size_y, out_rows, -1), "gy", 0, 0
    )
    copies = pl.pallas_call(
        finish_kernel,
        out_shape=jax.ShapeDtypeStruct(terms.shape, jnp.bfloat16),
        in_specs=[vmem, vmem],
        out_specs=vmem,
        compiler_params=pltpu.CompilerParams(vmem_limit_bytes=16 * 2**20),
        name="finish",
    )(kept, terms)
    mixed = lax.all_to_all(copies, "gy", 0, 0).reshape(all_rows, -1)
    return (mixed, new_state)


def solution(mesh):
    placed = (
        P(None, "gx"),
        P("gx"),
        P("gx", None, "gy"),
        P("gy", "gx"),
        P("gy"),
        P("gx", "gy", None, None),
    )
    return jax.shard_map(
        local,
        mesh=mesh,
        in_specs=placed,
        out_specs=(P(None, "gx"), P("gx", "gy", None, None)),
        check_vma=False,
    )
```

```python
import jax
import jax.numpy as jnp
from jax import lax
from jax.experimental import pallas as pl
from jax.experimental.pallas import tpu as pltpu
from jax.sharding import PartitionSpec as P

HS = 256
D = 8192
LANES = 128


def split_squares(squares):
    high = squares.astype(jnp.bfloat16).astype(jnp.float32)
    low = squares - high
    lane = lax.broadcasted_iota(jnp.int32, (squares.shape[0], LANES), 1)
    return jnp.where(lane == 0, high, jnp.where(lane == 1, low, 0.0))


def scale_kernel(
    tokens_hbm, gain_hbm, scaled_ref, away_squares_ref, own_squares_ref, kept_ref,
    tokens_ref, gain_ref, rows_ref, squares_ref, sems,
):
    loads = [
        pltpu.make_async_copy(tokens_hbm, tokens_ref, sems.at[0]),
        pltpu.make_async_copy(gain_hbm, gain_ref, sems.at[1]),
    ]
    for load in loads:
        load.start()
    for load in loads:
        load.wait()
    chips, _, rows, features = rows_ref.shape
    half = chips * rows
    core = lax.rem(lax.axis_index("gx"), 2)
    tokens = tokens_ref[...].astype(jnp.float32)
    squares = jnp.sum(tokens * tokens, axis=1, keepdims=True)
    rows_ref[...] = (tokens * gain_ref[...]).reshape(rows_ref.shape)
    squares_ref[...] = jnp.broadcast_to(squares, (tokens.shape[0], LANES)).reshape(squares_ref.shape)
    for n, (which, out_ref) in enumerate(
        ((1 - core, away_squares_ref), (core, own_squares_ref))
    ):
        x = rows_ref[:, which].reshape(half, features).astype(jnp.bfloat16)
        for p in range(scaled_ref.shape[0]):
            scaled_ref[p, n * half : (n + 1) * half] = x
        out_ref[...] = squares_ref[:, which].reshape(half, LANES)
    block = lax.axis_index("gy")
    kept = jnp.zeros(kept_ref.shape, jnp.float32)
    for y in range(tokens.shape[0] // kept.shape[0]):
        kept = jnp.where(block == y, tokens[y * kept.shape[0] : (y + 1) * kept.shape[0]], kept)
    kept_ref[...] = kept


def pair_kernel(products_ref, arrived_ref, own_ref, other_ref, state_ref, pair_ref):
    del state_ref
    kinds, half, width = arrived_ref.shape
    for p in range(kinds):
        pair_ref[:, p * width : (p + 1) * width] = (
            products_ref[p, half:].astype(jnp.float32) + arrived_ref[p].astype(jnp.float32)
        ).astype(jnp.bfloat16)
    total = (own_ref[...] + other_ref[...])[:, :1]
    pair_ref[:, kinds * width :] = split_squares(total).astype(jnp.bfloat16)


def readout_kernel(
    decay_ref, parts_ref, state_ref, copies_ref, keys_ref, values_ref, query_cols_ref
):
    pieces, rows, _ = parts_ref.shape
    heads = state_ref.shape[1]
    width = heads * HS
    summed = parts_ref[0].astype(jnp.float32)
    for z in range(1, pieces):
        summed += parts_ref[z].astype(jnp.float32)
    squares = summed[:, 4 * width : 4 * width + 1] + summed[:, 4 * width + 1 : 4 * width + 2]
    scale = lax.rsqrt(squares / D + 1e-06)
    projected = summed[:, : 4 * width] * scale
    queries = projected[:, :width]
    keys = projected[:, width : 2 * width] * HS ** (-0.5)
    values = projected[:, 2 * width : 3 * width]
    gates = projected[:, 3 * width : 4 * width]
    query_cols_ref[...] = queries.T
    keys_ref[...] = keys
    values_ref[...] = values
    from_state = [[] for _ in range(heads)]
    for s in range(rows):
        for h in range(heads):
            query_col = query_cols_ref[h * HS : (h + 1) * HS, s : s + 1]
            from_state[h].append(jnp.sum(query_col * state_ref[s, h], axis=0, keepdims=True))
    normed = []
    for h in range(heads):
        here = slice(h * HS, (h + 1) * HS)
        overlap = jnp.sum(queries[:, here] * keys[:, here], axis=1, keepdims=True)
        readout = (
            decay_ref[h] * jnp.concatenate(from_state[h], axis=0) + overlap * values[:, here]
        )
        centre = jnp.mean(readout, axis=1, keepdims=True)
        spread = jnp.mean((readout - centre) ** 2, axis=1, keepdims=True)
        normed.append((readout - centre) * lax.rsqrt(spread + 1e-05))
    gated = gates / (1.0 + jnp.exp(-gates)) * jnp.concatenate(normed, axis=1)
    copies_ref[...] = jnp.broadcast_to(gated.astype(jnp.bfloat16)[None], copies_ref.shape)


def update_kernel(
    decay_ref, keys_ref, values_ref, state_ref, new_ref,
    key_cols_ref, held_ref, fresh_ref, in_sems, out_sems,
):
    rows, heads = state_ref.shape[:2]
    loads = [
        pltpu.make_async_copy(state_ref.at[s], held_ref.at[s], in_sems.at[s]) for s in range(rows)
    ]
    stores = [
        pltpu.make_async_copy(fresh_ref.at[s], new_ref.at[s], out_sems.at[s]) for s in range(rows)
    ]
    for load in loads:
        load.start()
    key_cols_ref[...] = keys_ref[...].T
    for s in range(rows):
        loads[s].wait()
        for h in range(heads):
            key_col = key_cols_ref[h * HS : (h + 1) * HS, s : s + 1]
            value_row = values_ref[s : s + 1, h * HS : (h + 1) * HS]
            fresh_ref[s, h] = decay_ref[h] * held_ref[s, h] + key_col * value_row
        stores[s].start()
    for store in stores:
        store.wait()


def finish_kernel(kept_ref, terms_ref, copies_ref):
    total = terms_ref[0].astype(jnp.float32)
    for y in range(1, terms_ref.shape[0]):
        total += terms_ref[y].astype(jnp.float32)
    mixed = (kept_ref[...] + total).astype(jnp.bfloat16)
    copies_ref[...] = jnp.broadcast_to(mixed[None], copies_ref.shape)


def local(tokens, norm_gain, w_project, w_output, decay, state):
    all_rows, features = tokens.shape
    size_x, size_y = lax.axis_size("gx"), lax.axis_size("gy")
    chips = size_x // 2
    own_rows = all_rows // size_x
    out_rows = all_rows // size_y
    heads = state.shape[1]
    kinds, width = w_project.shape[1:]
    padded = kinds * width + LANES
    half = all_rows // 2
    vmem = pl.BlockSpec(memory_space=pltpu.VMEM)
    smem = pl.BlockSpec(memory_space=pltpu.SMEM)
    hbm = pl.BlockSpec(memory_space=pltpu.HBM)
    scaled, away_squares, own_squares, kept = pl.pallas_call(
        scale_kernel,
        out_shape=(
            pltpu.VMEM((kinds, all_rows, features), jnp.bfloat16),
            pltpu.VMEM((half, LANES), jnp.float32),
            pltpu.VMEM((half, LANES), jnp.float32),
            pltpu.VMEM((out_rows, features), jnp.float32),
        ),
        in_specs=[hbm, hbm],
        out_specs=(vmem, vmem, vmem, vmem),
        scratch_shapes=[
            pltpu.VMEM(tokens.shape, tokens.dtype),
            pltpu.VMEM((1, features), jnp.float32),
            pltpu.VMEM((chips, 2, own_rows, features), jnp.float32),
            pltpu.VMEM((chips, 2, own_rows, LANES), jnp.float32),
            pltpu.SemaphoreType.DMA((2,)),
        ],
        compiler_params=pltpu.CompilerParams(vmem_limit_bytes=16 * 2**20),
        cost_estimate=pl.CostEstimate(flops=2**33, bytes_accessed=2**18, transcendentals=0),
        name="scale",
    )(
        pltpu.with_memory_space_constraint(tokens, pltpu.HBM),
        pltpu.with_memory_space_constraint(norm_gain.reshape(1, -1), pltpu.HBM),
    )
    products = jnp.einsum(
        "psi,ipo->pso", scaled, w_project, preferred_element_type=jnp.float32
    ).astype(jnp.bfloat16)
    state_hbm = pltpu.with_memory_space_constraint(state, pltpu.HBM)
    swap = [(i, i ^ 1) for i in range(size_x)]
    other_squares = lax.ppermute(away_squares, "gx", swap)
    arrived = lax.ppermute(products[:, :half], "gx", swap)
    pair = pl.pallas_call(
        pair_kernel,
        out_shape=jax.ShapeDtypeStruct((half, padded), jnp.bfloat16),
        in_specs=[vmem, vmem, vmem, vmem, pl.BlockSpec(memory_space=pl.ANY)],
        out_specs=vmem,
        compiler_params=pltpu.CompilerParams(vmem_limit_bytes=16 * 2**20),
        name="pair",
    )(products, arrived, own_squares, other_squares, state)
    groups = [[2 * z + c for z in range(chips)] for c in range(2)]
    parts = lax.all_to_all(
        pair.reshape(chips, own_rows, -1), "gx", 0, 0, axis_index_groups=groups
    )
    copies, keys, values = pl.pallas_call(
        readout_kernel,
        out_shape=(
            jax.ShapeDtypeStruct((size_x, own_rows, heads * HS), jnp.bfloat16),
            jax.ShapeDtypeStruct((own_rows, heads * HS), jnp.float32),
            jax.ShapeDtypeStruct((own_rows, heads * HS), jnp.float32),
        ),
        in_specs=[smem, vmem, vmem],
        out_specs=(vmem, vmem, vmem),
        scratch_shapes=[pltpu.VMEM((heads * HS, own_rows), jnp.float32)],
        compiler_params=pltpu.CompilerParams(vmem_limit_bytes=24 * 2**20),
        name="readout",
    )(decay, parts, state)
    new_state = pl.pallas_call(
        update_kernel,
        out_shape=jax.ShapeDtypeStruct(state.shape, jnp.float32),
        in_specs=[smem, vmem, vmem, hbm],
        out_specs=hbm,
        scratch_shapes=[
            pltpu.VMEM((heads * HS, own_rows), jnp.float32),
            pltpu.VMEM(state.shape, jnp.float32),
            pltpu.VMEM(state.shape, jnp.float32),
            pltpu.SemaphoreType.DMA((own_rows,)),
            pltpu.SemaphoreType.DMA((own_rows,)),
        ],
        compiler_params=pltpu.CompilerParams(vmem_limit_bytes=24 * 2**20),
        cost_estimate=pl.CostEstimate(flops=2**22, bytes_accessed=2**23, transcendentals=0),
        name="update",
    )(decay, keys, values, state_hbm)
    all_gated = lax.all_to_all(copies, "gx", 0, 0).reshape(all_rows, -1)
    head_terms = jnp.dot(all_gated, w_output, preferred_element_type=jnp.float32)
    terms = lax.all_to_all(
        head_terms.astype(jnp.bfloat16).reshape(size_y, out_rows, -1), "gy", 0, 0
    )
    copies = pl.pallas_call(
        finish_kernel,
        out_shape=jax.ShapeDtypeStruct(terms.shape, jnp.bfloat16),
        in_specs=[vmem, vmem],
        out_specs=vmem,
        compiler_params=pltpu.CompilerParams(vmem_limit_bytes=16 * 2**20),
        name="finish",
    )(kept, terms)
    mixed = lax.all_to_all(copies, "gy", 0, 0).reshape(all_rows, -1)
    return (mixed, new_state)


def solution(mesh):
    placed = (
        P(None, "gx"),
        P("gx"),
        P("gx", None, "gy"),
        P("gy", "gx"),
        P("gy"),
        P("gx", "gy", None, None),
    )
    return jax.shard_map(
        local,
        mesh=mesh,
        in_specs=placed,
        out_specs=(P(None, "gx"), P("gx", "gy", None, None)),
        check_vma=False,
    )
```

```python
import jax
import jax.numpy as jnp
from jax import lax
from jax.experimental import pallas as pl
from jax.experimental.pallas import tpu as pltpu
from jax.sharding import PartitionSpec as P

HS = 256
D = 8192
LANES = 128


def split_squares(squares):
    high = squares.astype(jnp.bfloat16).astype(jnp.float32)
    low = squares - high
    lane = lax.broadcasted_iota(jnp.int32, (squares.shape[0], LANES), 1)
    return jnp.where(lane == 0, high, jnp.where(lane == 1, low, 0.0))


def scale_kernel(
    tokens_hbm, gain_hbm, scaled_ref, away_squares_ref, own_squares_ref,
    tokens_ref, gain_ref, rows_ref, squares_ref, sems,
):
    loads = [
        pltpu.make_async_copy(tokens_hbm, tokens_ref, sems.at[0]),
        pltpu.make_async_copy(gain_hbm, gain_ref, sems.at[1]),
    ]
    for load in loads:
        load.start()
    for load in loads:
        load.wait()
    chips, _, rows, features = rows_ref.shape
    half = chips * rows
    core = lax.rem(lax.axis_index("gx"), 2)
    tokens = tokens_ref[...].astype(jnp.float32)
    squares = jnp.sum(tokens * tokens, axis=1, keepdims=True)
    rows_ref[...] = (tokens * gain_ref[...]).reshape(rows_ref.shape)
    squares_ref[...] = jnp.broadcast_to(squares, (tokens.shape[0], LANES)).reshape(squares_ref.shape)
    for n, (which, out_ref) in enumerate(
        ((1 - core, away_squares_ref), (core, own_squares_ref))
    ):
        x = rows_ref[:, which].reshape(half, features).astype(jnp.bfloat16)
        for p in range(scaled_ref.shape[0]):
            scaled_ref[p, n * half : (n + 1) * half] = x
        out_ref[...] = squares_ref[:, which].reshape(half, LANES)


def pair_kernel(products_ref, arrived_ref, own_ref, other_ref, state_ref, pair_ref):
    del state_ref
    kinds, half, width = arrived_ref.shape
    for p in range(kinds):
        pair_ref[:, p * width : (p + 1) * width] = (
            products_ref[p, half:].astype(jnp.float32) + arrived_ref[p].astype(jnp.float32)
        ).astype(jnp.bfloat16)
    total = (own_ref[...] + other_ref[...])[:, :1]
    pair_ref[:, kinds * width :] = split_squares(total).astype(jnp.bfloat16)


def readout_kernel(
    decay_ref, parts_ref, state_ref, copies_ref, keys_ref, values_ref, query_cols_ref
):
    pieces, rows, _ = parts_ref.shape
    heads = state_ref.shape[1]
    width = heads * HS
    summed = parts_ref[0].astype(jnp.float32)
    for z in range(1, pieces):
        summed += parts_ref[z].astype(jnp.float32)
    squares = summed[:, 4 * width : 4 * width + 1] + summed[:, 4 * width + 1 : 4 * width + 2]
    scale = lax.rsqrt(squares / D + 1e-06)
    projected = summed[:, : 4 * width] * scale
    queries = projected[:, :width]
    keys = projected[:, width : 2 * width] * HS ** (-0.5)
    values = projected[:, 2 * width : 3 * width]
    gates = projected[:, 3 * width : 4 * width]
    query_cols_ref[...] = summed[:, :width].T
    keys_ref[...] = keys
    values_ref[...] = values
    from_state = [[] for _ in range(heads)]
    for s in range(rows):
        for h in range(heads):
            query_col = query_cols_ref[h * HS : (h + 1) * HS, s : s + 1]
            from_state[h].append(jnp.sum(query_col * state_ref[s, h], axis=0, keepdims=True))
    normed = []
    for h in range(heads):
        here = slice(h * HS, (h + 1) * HS)
        overlap = jnp.sum(queries[:, here] * keys[:, here], axis=1, keepdims=True)
        readout = (
            decay_ref[h] * scale * jnp.concatenate(from_state[h], axis=0)
            + overlap * values[:, here]
        )
        centre = jnp.mean(readout, axis=1, keepdims=True)
        spread = jnp.mean((readout - centre) ** 2, axis=1, keepdims=True)
        normed.append((readout - centre) * lax.rsqrt(spread + 1e-05))
    gated = gates / (1.0 + jnp.exp(-gates)) * jnp.concatenate(normed, axis=1)
    copies_ref[...] = jnp.broadcast_to(gated.astype(jnp.bfloat16)[None], copies_ref.shape)


def update_kernel(
    decay_ref, keys_ref, values_ref, state_ref, new_ref,
    key_cols_ref, held_ref, fresh_ref, in_sems, out_sems,
):
    rows, heads = state_ref.shape[:2]
    loads = [
        pltpu.make_async_copy(state_ref.at[s], held_ref.at[s], in_sems.at[s]) for s in range(rows)
    ]
    stores = [
        pltpu.make_async_copy(fresh_ref.at[s], new_ref.at[s], out_sems.at[s]) for s in range(rows)
    ]
    for load in loads:
        load.start()
    key_cols_ref[...] = keys_ref[...].T
    for s in range(rows):
        loads[s].wait()
        for h in range(heads):
            key_col = key_cols_ref[h * HS : (h + 1) * HS, s : s + 1]
            value_row = values_ref[s : s + 1, h * HS : (h + 1) * HS]
            fresh_ref[s, h] = decay_ref[h] * held_ref[s, h] + key_col * value_row
        stores[s].start()
    for store in stores:
        store.wait()


def middle_kernel(terms_ref, copies_ref):
    total = terms_ref[0].astype(jnp.float32)
    for n in range(1, terms_ref.shape[0]):
        total += terms_ref[n].astype(jnp.float32)
    copies_ref[...] = jnp.broadcast_to(total.astype(jnp.bfloat16)[None], copies_ref.shape)


def finish_kernel(tokens_ref, terms_ref, mixed_ref):
    blocks, rows, _ = terms_ref.shape
    blocks //= 2
    for n in range(blocks):
        here = slice(n * rows, (n + 1) * rows)
        total = terms_ref[n].astype(jnp.float32) + terms_ref[blocks + n].astype(jnp.float32)
        mixed_ref[here] = (tokens_ref[here].astype(jnp.float32) + total).astype(jnp.bfloat16)


def local(tokens, norm_gain, w_project, w_output, decay, state):
    all_rows, features = tokens.shape
    size_x, size_y = lax.axis_size("gx"), lax.axis_size("gy")
    chips = size_x // 2
    own_rows = all_rows // size_x
    heads = state.shape[1]
    kinds, width = w_project.shape[1:]
    padded = kinds * width + LANES
    half = all_rows // 2
    vmem = pl.BlockSpec(memory_space=pltpu.VMEM)
    smem = pl.BlockSpec(memory_space=pltpu.SMEM)
    hbm = pl.BlockSpec(memory_space=pltpu.HBM)
    scaled, away_squares, own_squares = pl.pallas_call(
        scale_kernel,
        out_shape=(
            pltpu.VMEM((kinds, all_rows, features), jnp.bfloat16),
            pltpu.VMEM((half, LANES), jnp.float32),
            pltpu.VMEM((half, LANES), jnp.float32),
        ),
        in_specs=[hbm, hbm],
        out_specs=(vmem, vmem, vmem),
        scratch_shapes=[
            pltpu.VMEM(tokens.shape, tokens.dtype),
            pltpu.VMEM((1, features), jnp.float32),
            pltpu.VMEM((chips, 2, own_rows, features), jnp.float32),
            pltpu.VMEM((chips, 2, own_rows, LANES), jnp.float32),
            pltpu.SemaphoreType.DMA((2,)),
        ],
        compiler_params=pltpu.CompilerParams(vmem_limit_bytes=16 * 2**20),
        cost_estimate=pl.CostEstimate(flops=2**33, bytes_accessed=2**18, transcendentals=0),
        name="scale",
    )(
        pltpu.with_memory_space_constraint(tokens, pltpu.HBM),
        pltpu.with_memory_space_constraint(norm_gain.reshape(1, -1), pltpu.HBM),
    )
    products = jnp.einsum(
        "psi,ipo->pso", scaled, w_project, preferred_element_type=jnp.float32
    ).astype(jnp.bfloat16)
    state_hbm = pltpu.with_memory_space_constraint(state, pltpu.HBM)
    swap = [(i, i ^ 1) for i in range(size_x)]
    other_squares = lax.ppermute(away_squares, "gx", swap)
    arrived = lax.ppermute(products[:, :half], "gx", swap)
    pair = pl.pallas_call(
        pair_kernel,
        out_shape=jax.ShapeDtypeStruct((half, padded), jnp.bfloat16),
        in_specs=[vmem, vmem, vmem, vmem, pl.BlockSpec(memory_space=pl.ANY)],
        out_specs=vmem,
        compiler_params=pltpu.CompilerParams(vmem_limit_bytes=16 * 2**20),
        name="pair",
    )(products, arrived, own_squares, other_squares, state)
    groups = [[2 * z + c for z in range(chips)] for c in range(2)]
    parts = lax.all_to_all(
        pair.reshape(chips, own_rows, -1), "gx", 0, 0, axis_index_groups=groups
    )
    copies, keys, values = pl.pallas_call(
        readout_kernel,
        out_shape=(
            jax.ShapeDtypeStruct((size_x, own_rows, heads * HS), jnp.bfloat16),
            jax.ShapeDtypeStruct((own_rows, heads * HS), jnp.float32),
            jax.ShapeDtypeStruct((own_rows, heads * HS), jnp.float32),
        ),
        in_specs=[smem, vmem, vmem],
        out_specs=(vmem, vmem, vmem),
        scratch_shapes=[pltpu.VMEM((heads * HS, own_rows), jnp.float32)],
        compiler_params=pltpu.CompilerParams(vmem_limit_bytes=24 * 2**20),
        name="readout",
    )(decay, parts, state)
    new_state = pl.pallas_call(
        update_kernel,
        out_shape=jax.ShapeDtypeStruct(state.shape, jnp.float32),
        in_specs=[smem, vmem, vmem, hbm],
        out_specs=hbm,
        scratch_shapes=[
            pltpu.VMEM((heads * HS, own_rows), jnp.float32),
            pltpu.VMEM(state.shape, jnp.float32),
            pltpu.VMEM(state.shape, jnp.float32),
            pltpu.SemaphoreType.DMA((own_rows,)),
            pltpu.SemaphoreType.DMA((own_rows,)),
        ],
        compiler_params=pltpu.CompilerParams(vmem_limit_bytes=24 * 2**20),
        cost_estimate=pl.CostEstimate(flops=2**22, bytes_accessed=2**23, transcendentals=0),
        name="update",
    )(decay, keys, values, state_hbm)
    all_gated = lax.all_to_all(copies, "gx", 0, 0).reshape(all_rows, -1)
    head_terms = jnp.dot(all_gated, w_output, preferred_element_type=jnp.float32)
    blocks = size_y // 2
    halves = [list(range(blocks)), list(range(blocks, size_y))]
    params = pltpu.CompilerParams(vmem_limit_bytes=16 * 2**20)
    terms = lax.all_to_all(
        head_terms.astype(jnp.bfloat16).reshape(blocks, all_rows // blocks, features),
        "gy", 0, 0, axis_index_groups=halves,
    )
    copies = pl.pallas_call(
        middle_kernel,
        out_shape=jax.ShapeDtypeStruct((size_y,) + terms.shape[1:], jnp.bfloat16),
        in_specs=[vmem],
        out_specs=vmem,
        compiler_params=params,
        name="middle",
    )(terms)
    mixed = pl.pallas_call(
        finish_kernel,
        out_shape=jax.ShapeDtypeStruct((all_rows, features), jnp.bfloat16),
        in_specs=[vmem, vmem],
        out_specs=vmem,
        compiler_params=params,
        name="finish",
    )(tokens, lax.all_to_all(copies, "gy", 0, 0))
    return (mixed, new_state)


def solution(mesh):
    placed = (
        P(None, "gx"),
        P("gx"),
        P("gx", None, "gy"),
        P("gy", "gx"),
        P("gy"),
        P("gx", "gy", None, None),
    )
    return jax.shard_map(
        local,
        mesh=mesh,
        in_specs=placed,
        out_specs=(P(None, "gx"), P("gx", "gy", None, None)),
        check_vma=False,
    )
```

```python
import jax
import jax.numpy as jnp
from jax import lax
from jax.experimental import pallas as pl
from jax.experimental.pallas import tpu as pltpu
from jax.sharding import PartitionSpec as P

HS = 256
D = 8192
LANES = 128


def split_squares(squares):
    high = squares.astype(jnp.bfloat16).astype(jnp.float32)
    low = squares - high
    lane = lax.broadcasted_iota(jnp.int32, (squares.shape[0], LANES), 1)
    return jnp.where(lane == 0, high, jnp.where(lane == 1, low, 0.0))


def scale_kernel(
    tokens_hbm, gain_hbm, scaled_ref, away_squares_ref, own_squares_ref,
    tokens_ref, gain_ref, rows_ref, squares_ref, sems,
):
    loads = [
        pltpu.make_async_copy(tokens_hbm, tokens_ref, sems.at[0]),
        pltpu.make_async_copy(gain_hbm, gain_ref, sems.at[1]),
    ]
    for load in loads:
        load.start()
    for load in loads:
        load.wait()
    chips, _, rows, features = rows_ref.shape
    half = chips * rows
    core = lax.rem(lax.axis_index("gx"), 2)
    tokens = tokens_ref[...].astype(jnp.float32)
    squares = jnp.sum(tokens * tokens, axis=1, keepdims=True)
    rows_ref[...] = (tokens * gain_ref[...]).reshape(rows_ref.shape)
    squares_ref[...] = jnp.broadcast_to(squares, (tokens.shape[0], LANES)).reshape(squares_ref.shape)
    for n, (which, out_ref) in enumerate(
        ((1 - core, away_squares_ref), (core, own_squares_ref))
    ):
        x = rows_ref[:, which].reshape(half, features).astype(jnp.bfloat16)
        for p in range(scaled_ref.shape[0]):
            scaled_ref[p, n * half : (n + 1) * half] = x
        out_ref[...] = squares_ref[:, which].reshape(half, LANES)


def pair_kernel(products_ref, arrived_ref, own_ref, other_ref, state_ref, pair_ref):
    del state_ref
    kinds, half, width = arrived_ref.shape
    for p in range(kinds):
        pair_ref[:, p * width : (p + 1) * width] = (
            products_ref[p, half:].astype(jnp.float32) + arrived_ref[p].astype(jnp.float32)
        ).astype(jnp.bfloat16)
    total = (own_ref[...] + other_ref[...])[:, :1]
    pair_ref[:, kinds * width :] = split_squares(total).astype(jnp.bfloat16)


def readout_kernel(
    decay_ref, parts_ref, state_ref, copies_ref, keys_ref, values_ref, query_cols_ref
):
    pieces, rows, _ = parts_ref.shape
    heads = state_ref.shape[1]
    width = heads * HS
    summed = parts_ref[0].astype(jnp.float32)
    for z in range(1, pieces):
        summed += parts_ref[z].astype(jnp.float32)
    squares = summed[:, 4 * width : 4 * width + 1] + summed[:, 4 * width + 1 : 4 * width + 2]
    scale = lax.rsqrt(squares / D + 1e-06)
    projected = summed[:, : 4 * width] * scale
    queries = projected[:, :width]
    keys = projected[:, width : 2 * width] * HS ** (-0.5)
    values = projected[:, 2 * width : 3 * width]
    gates = projected[:, 3 * width : 4 * width]
    query_cols_ref[...] = summed[:, :width].T
    keys_ref[...] = keys
    values_ref[...] = values
    from_state = [[] for _ in range(heads)]
    for s in range(rows):
        for h in range(heads):
            query_col = query_cols_ref[h * HS : (h + 1) * HS, s : s + 1]
            from_state[h].append(jnp.sum(query_col * state_ref[s, h], axis=0, keepdims=True))
    normed = []
    for h in range(heads):
        here = slice(h * HS, (h + 1) * HS)
        overlap = jnp.sum(queries[:, here] * keys[:, here], axis=1, keepdims=True)
        readout = (
            decay_ref[:, h : h + 1] * scale * jnp.concatenate(from_state[h], axis=0)
            + overlap * values[:, here]
        )
        centre = jnp.mean(readout, axis=1, keepdims=True)
        spread = jnp.mean((readout - centre) ** 2, axis=1, keepdims=True)
        normed.append((readout - centre) * lax.rsqrt(spread + 1e-05))
    gated = gates / (1.0 + jnp.exp(-gates)) * jnp.concatenate(normed, axis=1)
    copies_ref[...] = jnp.broadcast_to(gated.astype(jnp.bfloat16)[None], copies_ref.shape)


def update_kernel(
    decay_ref, keys_ref, values_ref, state_ref, new_ref,
    key_cols_ref, held_ref, fresh_ref, in_sems, out_sems,
):
    rows, heads = state_ref.shape[:2]
    loads = [
        pltpu.make_async_copy(state_ref.at[s], held_ref.at[s], in_sems.at[s]) for s in range(rows)
    ]
    stores = [
        pltpu.make_async_copy(fresh_ref.at[s], new_ref.at[s], out_sems.at[s]) for s in range(rows)
    ]
    for load in loads:
        load.start()
    key_cols_ref[...] = keys_ref[...].T
    for s in range(rows):
        loads[s].wait()
        for h in range(heads):
            key_col = key_cols_ref[h * HS : (h + 1) * HS, s : s + 1]
            value_row = values_ref[s : s + 1, h * HS : (h + 1) * HS]
            fresh_ref[s, h] = decay_ref[h] * held_ref[s, h] + key_col * value_row
        stores[s].start()
    for store in stores:
        store.wait()


def middle_kernel(terms_ref, copies_ref):
    total = terms_ref[0].astype(jnp.float32)
    for n in range(1, terms_ref.shape[0]):
        total += terms_ref[n].astype(jnp.float32)
    copies_ref[...] = jnp.broadcast_to(total.astype(jnp.bfloat16)[None], copies_ref.shape)


def finish_kernel(tokens_ref, terms_ref, mixed_ref):
    blocks, rows, _ = terms_ref.shape
    blocks //= 2
    for n in range(blocks):
        here = slice(n * rows, (n + 1) * rows)
        total = terms_ref[n].astype(jnp.float32) + terms_ref[blocks + n].astype(jnp.float32)
        mixed_ref[here] = (tokens_ref[here].astype(jnp.float32) + total).astype(jnp.bfloat16)


def local(tokens, norm_gain, w_project, w_output, decay, state):
    all_rows, features = tokens.shape
    size_x, size_y = lax.axis_size("gx"), lax.axis_size("gy")
    chips = size_x // 2
    own_rows = all_rows // size_x
    heads = state.shape[1]
    kinds, width = w_project.shape[1:]
    padded = kinds * width + LANES
    half = all_rows // 2
    vmem = pl.BlockSpec(memory_space=pltpu.VMEM)
    smem = pl.BlockSpec(memory_space=pltpu.SMEM)
    hbm = pl.BlockSpec(memory_space=pltpu.HBM)
    scaled, away_squares, own_squares = pl.pallas_call(
        scale_kernel,
        out_shape=(
            pltpu.VMEM((kinds, all_rows, features), jnp.bfloat16),
            pltpu.VMEM((half, LANES), jnp.float32),
            pltpu.VMEM((half, LANES), jnp.float32),
        ),
        in_specs=[hbm, hbm],
        out_specs=(vmem, vmem, vmem),
        scratch_shapes=[
            pltpu.VMEM(tokens.shape, tokens.dtype),
            pltpu.VMEM((1, features), jnp.float32),
            pltpu.VMEM((chips, 2, own_rows, features), jnp.float32),
            pltpu.VMEM((chips, 2, own_rows, LANES), jnp.float32),
            pltpu.SemaphoreType.DMA((2,)),
        ],
        compiler_params=pltpu.CompilerParams(vmem_limit_bytes=16 * 2**20),
        cost_estimate=pl.CostEstimate(flops=2**33, bytes_accessed=2**18, transcendentals=0),
        name="scale",
    )(
        pltpu.with_memory_space_constraint(tokens, pltpu.HBM),
        pltpu.with_memory_space_constraint(norm_gain.reshape(1, -1), pltpu.HBM),
    )
    products = jnp.einsum(
        "psi,ipo->pso", scaled, w_project, preferred_element_type=jnp.float32
    ).astype(jnp.bfloat16)
    state_hbm = pltpu.with_memory_space_constraint(state, pltpu.HBM)
    swap = [(i, i ^ 1) for i in range(size_x)]
    other_squares = lax.ppermute(away_squares, "gx", swap)
    arrived = lax.ppermute(products[:, :half], "gx", swap)
    pair = pl.pallas_call(
        pair_kernel,
        out_shape=jax.ShapeDtypeStruct((half, padded), jnp.bfloat16),
        in_specs=[vmem, vmem, vmem, vmem, pl.BlockSpec(memory_space=pl.ANY)],
        out_specs=vmem,
        compiler_params=pltpu.CompilerParams(vmem_limit_bytes=16 * 2**20),
        name="pair",
    )(products, arrived, own_squares, other_squares, state)
    groups = [[2 * z + c for z in range(chips)] for c in range(2)]
    parts = lax.all_to_all(
        pair.reshape(chips, own_rows, -1), "gx", 0, 0, axis_index_groups=groups
    )
    copies, keys, values = pl.pallas_call(
        readout_kernel,
        out_shape=(
            jax.ShapeDtypeStruct((size_x, own_rows, heads * HS), jnp.bfloat16),
            jax.ShapeDtypeStruct((own_rows, heads * HS), jnp.float32),
            jax.ShapeDtypeStruct((own_rows, heads * HS), jnp.float32),
        ),
        in_specs=[vmem, vmem, vmem],
        out_specs=(vmem, vmem, vmem),
        scratch_shapes=[pltpu.VMEM((heads * HS, own_rows), jnp.float32)],
        compiler_params=pltpu.CompilerParams(vmem_limit_bytes=24 * 2**20),
        name="readout",
    )(decay.reshape(1, heads), parts, state)
    new_state = pl.pallas_call(
        update_kernel,
        out_shape=jax.ShapeDtypeStruct(state.shape, jnp.float32),
        in_specs=[smem, vmem, vmem, hbm],
        out_specs=hbm,
        scratch_shapes=[
            pltpu.VMEM((heads * HS, own_rows), jnp.float32),
            pltpu.VMEM(state.shape, jnp.float32),
            pltpu.VMEM(state.shape, jnp.float32),
            pltpu.SemaphoreType.DMA((own_rows,)),
            pltpu.SemaphoreType.DMA((own_rows,)),
        ],
        compiler_params=pltpu.CompilerParams(vmem_limit_bytes=24 * 2**20),
        cost_estimate=pl.CostEstimate(flops=2**22, bytes_accessed=2**23, transcendentals=0),
        name="update",
    )(decay, keys, values, state_hbm)
    all_gated = lax.all_to_all(copies, "gx", 0, 0).reshape(all_rows, -1)
    head_terms = jnp.dot(all_gated, w_output, preferred_element_type=jnp.float32)
    blocks = size_y // 2
    halves = [list(range(blocks)), list(range(blocks, size_y))]
    params = pltpu.CompilerParams(vmem_limit_bytes=16 * 2**20)
    terms = lax.all_to_all(
        head_terms.astype(jnp.bfloat16).reshape(blocks, all_rows // blocks, features),
        "gy", 0, 0, axis_index_groups=halves,
    )
    copies = pl.pallas_call(
        middle_kernel,
        out_shape=jax.ShapeDtypeStruct((size_y,) + terms.shape[1:], jnp.bfloat16),
        in_specs=[vmem],
        out_specs=vmem,
        compiler_params=params,
        name="middle",
    )(terms)
    mixed = pl.pallas_call(
        finish_kernel,
        out_shape=jax.ShapeDtypeStruct((all_rows, features), jnp.bfloat16),
        in_specs=[vmem, vmem],
        out_specs=vmem,
        compiler_params=params,
        name="finish",
    )(tokens, lax.all_to_all(copies, "gy", 0, 0))
    return (mixed, new_state)


def solution(mesh):
    placed = (
        P(None, "gx"),
        P("gx"),
        P("gx", None, "gy"),
        P("gy", "gx"),
        P("gy"),
        P("gx", "gy", None, None),
    )
    return jax.shard_map(
        local,
        mesh=mesh,
        in_specs=placed,
        out_specs=(P(None, "gx"), P("gx", "gy", None, None)),
        check_vma=False,
    )
```

```python
import jax
import jax.numpy as jnp
from jax import lax
from jax.experimental import pallas as pl
from jax.experimental.pallas import tpu as pltpu
from jax.sharding import PartitionSpec as P

HS = 256
D = 8192
LANES = 128


def split_squares(squares):
    high = squares.astype(jnp.bfloat16).astype(jnp.float32)
    low = squares - high
    lane = lax.broadcasted_iota(jnp.int32, (squares.shape[0], LANES), 1)
    return jnp.where(lane == 0, high, jnp.where(lane == 1, low, 0.0))


def scale_kernel(
    tokens_hbm, gain_hbm, scaled_ref, away_squares_ref, own_squares_ref,
    tokens_ref, gain_ref, rows_ref, squares_ref, sems,
):
    loads = [
        pltpu.make_async_copy(tokens_hbm, tokens_ref, sems.at[0]),
        pltpu.make_async_copy(gain_hbm, gain_ref, sems.at[1]),
    ]
    for load in loads:
        load.start()
    for load in loads:
        load.wait()
    chips, _, rows, features = rows_ref.shape
    half = chips * rows
    core = lax.rem(lax.axis_index("gx"), 2)
    tokens = tokens_ref[...].astype(jnp.float32)
    squares = jnp.sum(tokens * tokens, axis=1, keepdims=True)
    rows_ref[...] = (tokens * gain_ref[...]).reshape(rows_ref.shape)
    squares_ref[...] = jnp.broadcast_to(squares, (tokens.shape[0], LANES)).reshape(squares_ref.shape)
    for n, (which, out_ref) in enumerate(
        ((1 - core, away_squares_ref), (core, own_squares_ref))
    ):
        x = rows_ref[:, which].reshape(half, features).astype(jnp.bfloat16)
        for p in range(scaled_ref.shape[0]):
            scaled_ref[p, n * half : (n + 1) * half] = x
        out_ref[...] = squares_ref[:, which].reshape(half, LANES)


def pair_kernel(products_ref, arrived_ref, own_ref, other_ref, state_ref, pair_ref):
    del state_ref
    kinds, half, width = arrived_ref.shape
    for p in range(kinds):
        pair_ref[:, p * width : (p + 1) * width] = (
            products_ref[p, half:].astype(jnp.float32) + arrived_ref[p].astype(jnp.float32)
        ).astype(jnp.bfloat16)
    total = (own_ref[...] + other_ref[...])[:, :1]
    pair_ref[:, kinds * width :] = split_squares(total).astype(jnp.bfloat16)


def readout_kernel(
    decay_ref, parts_ref, state_ref, copies_ref, keys_ref, values_ref, query_cols_ref
):
    pieces, rows, _ = parts_ref.shape
    heads = state_ref.shape[1]
    width = heads * HS
    summed = parts_ref[0].astype(jnp.float32)
    for z in range(1, pieces):
        summed += parts_ref[z].astype(jnp.float32)
    squares = summed[:, 4 * width : 4 * width + 1] + summed[:, 4 * width + 1 : 4 * width + 2]
    scale = lax.rsqrt(squares / D + 1e-06)
    projected = summed[:, : 4 * width] * scale
    queries = projected[:, :width]
    keys = projected[:, width : 2 * width] * HS ** (-0.5)
    values = projected[:, 2 * width : 3 * width]
    gates = projected[:, 3 * width : 4 * width]
    query_cols_ref[...] = summed[:, :width].T
    keys_ref[...] = keys
    values_ref[...] = values
    from_state = [[] for _ in range(heads)]
    for s in range(rows):
        for h in range(heads):
            query_col = query_cols_ref[h * HS : (h + 1) * HS, s : s + 1]
            from_state[h].append(jnp.sum(query_col * state_ref[s, h], axis=0, keepdims=True))
    normed = []
    for h in range(heads):
        here = slice(h * HS, (h + 1) * HS)
        overlap = jnp.sum(queries[:, here] * keys[:, here], axis=1, keepdims=True)
        readout = (
            decay_ref[:, h : h + 1] * scale * jnp.concatenate(from_state[h], axis=0)
            + overlap * values[:, here]
        )
        centre = jnp.mean(readout, axis=1, keepdims=True)
        spread = jnp.mean((readout - centre) ** 2, axis=1, keepdims=True)
        normed.append((readout - centre) * lax.rsqrt(spread + 1e-05))
    gated = gates / (1.0 + jnp.exp(-gates)) * jnp.concatenate(normed, axis=1)
    copies_ref[...] = jnp.broadcast_to(gated.astype(jnp.bfloat16)[None], copies_ref.shape)


def update_kernel(
    decay_ref, keys_ref, values_ref, state_ref, new_ref,
    key_cols_ref, held_ref, fresh_ref, in_sems, out_sems,
):
    rows, heads = state_ref.shape[:2]
    loads = [
        pltpu.make_async_copy(state_ref.at[s], held_ref.at[s], in_sems.at[s]) for s in range(rows)
    ]
    stores = [
        pltpu.make_async_copy(fresh_ref.at[s], new_ref.at[s], out_sems.at[s]) for s in range(rows)
    ]
    for load in loads:
        load.start()
    key_cols_ref[...] = keys_ref[...].T
    for s in range(rows):
        loads[s].wait()
        for h in range(heads):
            key_col = key_cols_ref[h * HS : (h + 1) * HS, s : s + 1]
            value_row = values_ref[s : s + 1, h * HS : (h + 1) * HS]
            fresh_ref[s, h] = decay_ref[h] * held_ref[s, h] + key_col * value_row
        stores[s].start()
    for store in stores:
        store.wait()


def middle_kernel(terms_ref, copies_ref):
    total = terms_ref[0].astype(jnp.float32)
    for n in range(1, terms_ref.shape[0]):
        total += terms_ref[n].astype(jnp.float32)
    copies_ref[...] = jnp.broadcast_to(total.astype(jnp.bfloat16)[None], copies_ref.shape)


def finish_kernel(tokens_ref, terms_ref, mixed_ref):
    rows = terms_ref.shape[1]
    for y in range(2):
        for x in range(2):
            n = 2 * y + x
            here = slice(n * rows, (n + 1) * rows)
            total = terms_ref[4 * y + x].astype(jnp.float32)
            total += terms_ref[4 * y + 2 + x].astype(jnp.float32)
            mixed_ref[here] = (tokens_ref[here].astype(jnp.float32) + total).astype(jnp.bfloat16)


def local(tokens, norm_gain, w_project, w_output, decay, state):
    all_rows, features = tokens.shape
    size_x = lax.axis_size("gx")
    chips = size_x // 2
    own_rows = all_rows // size_x
    heads = state.shape[1]
    kinds, width = w_project.shape[1:]
    padded = kinds * width + LANES
    half = all_rows // 2
    vmem = pl.BlockSpec(memory_space=pltpu.VMEM)
    smem = pl.BlockSpec(memory_space=pltpu.SMEM)
    hbm = pl.BlockSpec(memory_space=pltpu.HBM)
    scaled, away_squares, own_squares = pl.pallas_call(
        scale_kernel,
        out_shape=(
            pltpu.VMEM((kinds, all_rows, features), jnp.bfloat16),
            pltpu.VMEM((half, LANES), jnp.float32),
            pltpu.VMEM((half, LANES), jnp.float32),
        ),
        in_specs=[hbm, hbm],
        out_specs=(vmem, vmem, vmem),
        scratch_shapes=[
            pltpu.VMEM(tokens.shape, tokens.dtype),
            pltpu.VMEM((1, features), jnp.float32),
            pltpu.VMEM((chips, 2, own_rows, features), jnp.float32),
            pltpu.VMEM((chips, 2, own_rows, LANES), jnp.float32),
            pltpu.SemaphoreType.DMA((2,)),
        ],
        compiler_params=pltpu.CompilerParams(vmem_limit_bytes=16 * 2**20),
        cost_estimate=pl.CostEstimate(flops=2**33, bytes_accessed=2**18, transcendentals=0),
        name="scale",
    )(
        pltpu.with_memory_space_constraint(tokens, pltpu.HBM),
        pltpu.with_memory_space_constraint(norm_gain.reshape(1, -1), pltpu.HBM),
    )
    products = jnp.einsum(
        "psi,ipo->pso", scaled, w_project, preferred_element_type=jnp.float32
    ).astype(jnp.bfloat16)
    state_hbm = pltpu.with_memory_space_constraint(state, pltpu.HBM)
    swap = [(i, i ^ 1) for i in range(size_x)]
    other_squares = lax.ppermute(away_squares, "gx", swap)
    arrived = lax.ppermute(products[:, :half], "gx", swap)
    pair = pl.pallas_call(
        pair_kernel,
        out_shape=jax.ShapeDtypeStruct((half, padded), jnp.bfloat16),
        in_specs=[vmem, vmem, vmem, vmem, pl.BlockSpec(memory_space=pl.ANY)],
        out_specs=vmem,
        compiler_params=pltpu.CompilerParams(vmem_limit_bytes=16 * 2**20),
        name="pair",
    )(products, arrived, own_squares, other_squares, state)
    groups = [[2 * z + c for z in range(chips)] for c in range(2)]
    parts = lax.all_to_all(
        pair.reshape(chips, own_rows, -1), "gx", 0, 0, axis_index_groups=groups
    )
    copies, keys, values = pl.pallas_call(
        readout_kernel,
        out_shape=(
            jax.ShapeDtypeStruct((size_x, own_rows, heads * HS), jnp.bfloat16),
            jax.ShapeDtypeStruct((own_rows, heads * HS), jnp.float32),
            jax.ShapeDtypeStruct((own_rows, heads * HS), jnp.float32),
        ),
        in_specs=[vmem, vmem, vmem],
        out_specs=(vmem, vmem, vmem),
        scratch_shapes=[pltpu.VMEM((heads * HS, own_rows), jnp.float32)],
        compiler_params=pltpu.CompilerParams(vmem_limit_bytes=24 * 2**20),
        name="readout",
    )(decay.reshape(1, heads), parts, state)
    new_state = pl.pallas_call(
        update_kernel,
        out_shape=jax.ShapeDtypeStruct(state.shape, jnp.float32),
        in_specs=[smem, vmem, vmem, hbm],
        out_specs=hbm,
        scratch_shapes=[
            pltpu.VMEM((heads * HS, own_rows), jnp.float32),
            pltpu.VMEM(state.shape, jnp.float32),
            pltpu.VMEM(state.shape, jnp.float32),
            pltpu.SemaphoreType.DMA((own_rows,)),
            pltpu.SemaphoreType.DMA((own_rows,)),
        ],
        compiler_params=pltpu.CompilerParams(vmem_limit_bytes=24 * 2**20),
        cost_estimate=pl.CostEstimate(flops=2**22, bytes_accessed=2**23, transcendentals=0),
        name="update",
    )(decay, keys, values, state_hbm)
    all_gated = lax.all_to_all(copies, "gx", 0, 0).reshape(all_rows, -1)
    head_terms = jnp.dot(all_gated, w_output, preferred_element_type=jnp.float32)
    by_x = [[4 * y + 2 * h + x for y in range(4) for x in range(2)] for h in range(2)]
    by_y = [[4 * (2 * h + y) + x for y in range(2) for x in range(4)] for h in range(2)]
    params = pltpu.CompilerParams(vmem_limit_bytes=16 * 2**20)
    pieces = head_terms.astype(jnp.bfloat16).reshape(1, 4, all_rows // 4, features)
    pieces = jnp.broadcast_to(pieces, (2,) + pieces.shape[1:]).reshape((8,) + pieces.shape[2:])
    terms = lax.all_to_all(pieces, "gy", 0, 0, axis_index_groups=by_x)
    copies = pl.pallas_call(
        middle_kernel,
        out_shape=jax.ShapeDtypeStruct(terms.shape, jnp.bfloat16),
        in_specs=[vmem],
        out_specs=vmem,
        compiler_params=params,
        name="middle",
    )(terms)
    mixed = pl.pallas_call(
        finish_kernel,
        out_shape=jax.ShapeDtypeStruct((all_rows, features), jnp.bfloat16),
        in_specs=[vmem, vmem],
        out_specs=vmem,
        compiler_params=params,
        name="finish",
    )(tokens, lax.all_to_all(copies, "gy", 0, 0, axis_index_groups=by_y))
    return (mixed, new_state)


def solution(mesh):
    placed = (
        P(None, "gx"),
        P("gx"),
        P("gx", None, "gy"),
        P("gy", "gx"),
        P("gy"),
        P("gx", "gy", None, None),
    )
    return jax.shard_map(
        local,
        mesh=mesh,
        in_specs=placed,
        out_specs=(P(None, "gx"), P("gx", "gy", None, None)),
        check_vma=False,
    )
```

```python
import jax
import jax.numpy as jnp
from jax import lax
from jax.experimental import pallas as pl
from jax.experimental.pallas import tpu as pltpu
from jax.sharding import PartitionSpec as P

HS = 256
D = 8192
LANES = 128


def split_squares(squares):
    high = squares.astype(jnp.bfloat16).astype(jnp.float32)
    low = squares - high
    lane = lax.broadcasted_iota(jnp.int32, (squares.shape[0], LANES), 1)
    return jnp.where(lane == 0, high, jnp.where(lane == 1, low, 0.0))


def scale_kernel(
    tokens_hbm, gain_hbm, scaled_ref, away_squares_ref, own_squares_ref,
    tokens_ref, gain_ref, rows_ref, squares_ref, sems,
):
    loads = [
        pltpu.make_async_copy(tokens_hbm, tokens_ref, sems.at[0]),
        pltpu.make_async_copy(gain_hbm, gain_ref, sems.at[1]),
    ]
    for load in loads:
        load.start()
    for load in loads:
        load.wait()
    chips, _, rows, features = rows_ref.shape
    half = chips * rows
    core = lax.rem(lax.axis_index("gx"), 2)
    tokens = tokens_ref[...].astype(jnp.float32)
    squares = jnp.sum(tokens * tokens, axis=1, keepdims=True)
    rows_ref[...] = (tokens * gain_ref[...]).reshape(rows_ref.shape)
    squares_ref[...] = jnp.broadcast_to(squares, (tokens.shape[0], LANES)).reshape(squares_ref.shape)
    for n, (which, out_ref) in enumerate(
        ((1 - core, away_squares_ref), (core, own_squares_ref))
    ):
        x = rows_ref[:, which].reshape(half, features).astype(jnp.bfloat16)
        for p in range(scaled_ref.shape[0]):
            scaled_ref[p, n * half : (n + 1) * half] = x
        out_ref[...] = squares_ref[:, which].reshape(half, LANES)


def pair_kernel(products_ref, arrived_ref, own_ref, other_ref, state_ref, pair_ref):
    del state_ref
    kinds, half, width = arrived_ref.shape
    for p in range(kinds):
        pair_ref[:, p * width : (p + 1) * width] = (
            products_ref[p, half:].astype(jnp.float32) + arrived_ref[p].astype(jnp.float32)
        ).astype(jnp.bfloat16)
    total = (own_ref[...] + other_ref[...])[:, :1]
    pair_ref[:, kinds * width :] = split_squares(total).astype(jnp.bfloat16)


def readout_kernel(
    decay_ref, parts_ref, state_ref, copies_ref, keys_ref, values_ref, query_cols_ref
):
    pieces, rows, _ = parts_ref.shape
    heads = state_ref.shape[1]
    width = heads * HS
    summed = parts_ref[0].astype(jnp.float32)
    for z in range(1, pieces):
        summed += parts_ref[z].astype(jnp.float32)
    squares = summed[:, 4 * width : 4 * width + 1] + summed[:, 4 * width + 1 : 4 * width + 2]
    scale = lax.rsqrt(squares / D + 1e-06)
    projected = summed[:, : 4 * width] * scale
    queries = projected[:, :width]
    keys = projected[:, width : 2 * width] * HS ** (-0.5)
    values = projected[:, 2 * width : 3 * width]
    gates = projected[:, 3 * width : 4 * width]
    query_cols_ref[...] = summed[:, :width].T
    keys_ref[...] = keys
    values_ref[...] = values
    from_state = [[] for _ in range(heads)]
    for s in range(rows):
        for h in range(heads):
            query_col = query_cols_ref[h * HS : (h + 1) * HS, s : s + 1]
            from_state[h].append(jnp.sum(query_col * state_ref[s, h], axis=0, keepdims=True))
    normed = []
    for h in range(heads):
        here = slice(h * HS, (h + 1) * HS)
        overlap = jnp.sum(queries[:, here] * keys[:, here], axis=1, keepdims=True)
        readout = (
            decay_ref[:, h : h + 1] * scale * jnp.concatenate(from_state[h], axis=0)
            + overlap * values[:, here]
        )
        centre = jnp.mean(readout, axis=1, keepdims=True)
        spread = jnp.mean((readout - centre) ** 2, axis=1, keepdims=True)
        normed.append((readout - centre) * lax.rsqrt(spread + 1e-05))
    gated = gates / (1.0 + jnp.exp(-gates)) * jnp.concatenate(normed, axis=1)
    copies_ref[...] = jnp.broadcast_to(gated.astype(jnp.bfloat16)[None], copies_ref.shape)


def update_kernel(
    decay_ref, keys_ref, values_ref, state_ref, new_ref,
    key_cols_ref, held_ref, fresh_ref, in_sems, out_sems,
):
    rows, heads = state_ref.shape[:2]
    loads = [
        pltpu.make_async_copy(state_ref.at[s], held_ref.at[s], in_sems.at[s]) for s in range(rows)
    ]
    stores = [
        pltpu.make_async_copy(fresh_ref.at[s], new_ref.at[s], out_sems.at[s]) for s in range(rows)
    ]
    for load in loads:
        load.start()
    key_cols_ref[...] = keys_ref[...].T
    for s in range(rows):
        loads[s].wait()
        for h in range(heads):
            key_col = key_cols_ref[h * HS : (h + 1) * HS, s : s + 1]
            value_row = values_ref[s : s + 1, h * HS : (h + 1) * HS]
            decay = decay_ref[:, h : h + 1]
            fresh_ref[s, h] = decay * held_ref[s, h] + key_col * value_row
        stores[s].start()
    for store in stores:
        store.wait()


def middle_kernel(terms_ref, copies_ref):
    total = terms_ref[0].astype(jnp.float32)
    for n in range(1, terms_ref.shape[0]):
        total += terms_ref[n].astype(jnp.float32)
    copies_ref[...] = jnp.broadcast_to(total.astype(jnp.bfloat16)[None], copies_ref.shape)


def finish_kernel(tokens_ref, terms_ref, mixed_ref):
    rows = terms_ref.shape[1]
    for y in range(2):
        for x in range(2):
            n = 2 * y + x
            here = slice(n * rows, (n + 1) * rows)
            total = terms_ref[4 * y + x].astype(jnp.float32)
            total += terms_ref[4 * y + 2 + x].astype(jnp.float32)
            mixed_ref[here] = (tokens_ref[here].astype(jnp.float32) + total).astype(jnp.bfloat16)


def local(tokens, norm_gain, w_project, w_output, decay, state):
    all_rows, features = tokens.shape
    size_x = lax.axis_size("gx")
    chips = size_x // 2
    own_rows = all_rows // size_x
    heads = state.shape[1]
    kinds, width = w_project.shape[1:]
    padded = kinds * width + LANES
    half = all_rows // 2
    vmem = pl.BlockSpec(memory_space=pltpu.VMEM)
    hbm = pl.BlockSpec(memory_space=pltpu.HBM)
    scaled, away_squares, own_squares = pl.pallas_call(
        scale_kernel,
        out_shape=(
            pltpu.VMEM((kinds, all_rows, features), jnp.bfloat16),
            pltpu.VMEM((half, LANES), jnp.float32),
            pltpu.VMEM((half, LANES), jnp.float32),
        ),
        in_specs=[hbm, hbm],
        out_specs=(vmem, vmem, vmem),
        scratch_shapes=[
            pltpu.VMEM(tokens.shape, tokens.dtype),
            pltpu.VMEM((1, features), jnp.float32),
            pltpu.VMEM((chips, 2, own_rows, features), jnp.float32),
            pltpu.VMEM((chips, 2, own_rows, LANES), jnp.float32),
            pltpu.SemaphoreType.DMA((2,)),
        ],
        compiler_params=pltpu.CompilerParams(vmem_limit_bytes=16 * 2**20),
        cost_estimate=pl.CostEstimate(flops=2**33, bytes_accessed=2**18, transcendentals=0),
        name="scale",
    )(
        pltpu.with_memory_space_constraint(tokens, pltpu.HBM),
        pltpu.with_memory_space_constraint(norm_gain.reshape(1, -1), pltpu.HBM),
    )
    products = jnp.einsum(
        "psi,ipo->pso", scaled, w_project, preferred_element_type=jnp.float32
    ).astype(jnp.bfloat16)
    state_hbm = pltpu.with_memory_space_constraint(state, pltpu.HBM)
    swap = [(i, i ^ 1) for i in range(size_x)]
    other_squares = lax.ppermute(away_squares, "gx", swap)
    arrived = lax.ppermute(products[:, :half], "gx", swap)
    pair = pl.pallas_call(
        pair_kernel,
        out_shape=jax.ShapeDtypeStruct((half, padded), jnp.bfloat16),
        in_specs=[vmem, vmem, vmem, vmem, pl.BlockSpec(memory_space=pl.ANY)],
        out_specs=vmem,
        compiler_params=pltpu.CompilerParams(vmem_limit_bytes=16 * 2**20),
        name="pair",
    )(products, arrived, own_squares, other_squares, state)
    groups = [[2 * z + c for z in range(chips)] for c in range(2)]
    parts = lax.all_to_all(
        pair.reshape(chips, own_rows, -1), "gx", 0, 0, axis_index_groups=groups
    )
    copies, keys, values = pl.pallas_call(
        readout_kernel,
        out_shape=(
            jax.ShapeDtypeStruct((size_x, own_rows, heads * HS), jnp.bfloat16),
            jax.ShapeDtypeStruct((own_rows, heads * HS), jnp.float32),
            jax.ShapeDtypeStruct((own_rows, heads * HS), jnp.float32),
        ),
        in_specs=[vmem, vmem, vmem],
        out_specs=(vmem, vmem, vmem),
        scratch_shapes=[pltpu.VMEM((heads * HS, own_rows), jnp.float32)],
        compiler_params=pltpu.CompilerParams(vmem_limit_bytes=24 * 2**20),
        name="readout",
    )(decay.reshape(1, heads), parts, state)
    new_state = pl.pallas_call(
        update_kernel,
        out_shape=jax.ShapeDtypeStruct(state.shape, jnp.float32),
        in_specs=[vmem, vmem, vmem, hbm],
        out_specs=hbm,
        scratch_shapes=[
            pltpu.VMEM((heads * HS, own_rows), jnp.float32),
            pltpu.VMEM(state.shape, jnp.float32),
            pltpu.VMEM(state.shape, jnp.float32),
            pltpu.SemaphoreType.DMA((own_rows,)),
            pltpu.SemaphoreType.DMA((own_rows,)),
        ],
        compiler_params=pltpu.CompilerParams(vmem_limit_bytes=24 * 2**20),
        cost_estimate=pl.CostEstimate(flops=2**22, bytes_accessed=2**23, transcendentals=0),
        name="update",
    )(decay.reshape(1, heads), keys, values, state_hbm)
    all_gated = lax.all_to_all(copies, "gx", 0, 0).reshape(all_rows, -1)
    head_terms = jnp.dot(all_gated, w_output, preferred_element_type=jnp.float32)
    by_x = [[4 * y + 2 * h + x for y in range(4) for x in range(2)] for h in range(2)]
    by_y = [[4 * (2 * h + y) + x for y in range(2) for x in range(4)] for h in range(2)]
    params = pltpu.CompilerParams(vmem_limit_bytes=16 * 2**20)
    pieces = head_terms.astype(jnp.bfloat16).reshape(1, 4, all_rows // 4, features)
    pieces = jnp.broadcast_to(pieces, (2,) + pieces.shape[1:]).reshape((8,) + pieces.shape[2:])
    terms = lax.all_to_all(pieces, "gy", 0, 0, axis_index_groups=by_x)
    copies = pl.pallas_call(
        middle_kernel,
        out_shape=jax.ShapeDtypeStruct(terms.shape, jnp.bfloat16),
        in_specs=[vmem],
        out_specs=vmem,
        compiler_params=params,
        name="middle",
    )(terms)
    mixed = pl.pallas_call(
        finish_kernel,
        out_shape=jax.ShapeDtypeStruct((all_rows, features), jnp.bfloat16),
        in_specs=[vmem, vmem],
        out_specs=vmem,
        compiler_params=params,
        name="finish",
    )(tokens, lax.all_to_all(copies, "gy", 0, 0, axis_index_groups=by_y))
    return (mixed, new_state)


def solution(mesh):
    placed = (
        P(None, "gx"),
        P("gx"),
        P("gx", None, "gy"),
        P("gy", "gx"),
        P("gy"),
        P("gx", "gy", None, None),
    )
    return jax.shard_map(
        local,
        mesh=mesh,
        in_specs=placed,
        out_specs=(P(None, "gx"), P("gx", "gy", None, None)),
        check_vma=False,
    )
```
